128 devices in a mesh: depth: 4 (over y_hi, core), row: 4 (over z), col: 8 (over x, y_lo).
Axes of the slice: x: 4, y: 4 (y_hi: 2, y_lo: 2; y = y_hi * 2 + y_lo), z: 4, core: 2. Of those that a mesh axis runs over, the one named last changes fastest.
Arguments:
- left_factor: bfloat16 [1792, 32, 512], P('depth', None, 'row'), may hold values from -6 to 6
- right_factor: bfloat16 [1792, 32, 512], P('depth', None, 'col'), may hold values from -6 to 6
- out_weight: bfloat16 [1024, 128], replicated, may hold values from -12 to 12
- pair_cotangent: bfloat16 [512, 512, 128], P(('row', 'depth'), 'col'), may hold values from -0.29882812 to 0.29882812
Outputs:
- left_grad: float32 [1792, 32, 512], P(('depth', 'col'), None, 'row')
- right_grad: float32 [1792, 32, 512], P(('depth', 'row'), None, 'col')
- weight_grad: float32 [1024, 128], P(('depth', 'row', 'col'))
The draws below stay inside these ranges and needn't reach their ends.
All inputs are finite; a program needn't handle non-finite values.
Results may differ from the reference program's by a relative error of at most 0.0075.
Values may be sent and summed in bfloat16 or wider, within the bound.
No kernel may reach another device: no remote copies, remote signals or barrier semaphores. Data moves between devices by JAX's collectives and lax.ppermute only.
A program may use at most 256 MiB of HBM per device.

```python
import jax
import jax.numpy as jnp
from jax import lax

C = 32
P_SIZE = 128
TOK_ROW = 128
CC = 1024
S = 1792
N = 512


def block_scale(rng, dims, split, smallest, largest):
    gain = 1.0
    for axis_at, blocks in split:
        heights = jax.random.uniform(jax.random.fold_in(jax.random.fold_in(rng, 6), axis_at), (blocks,), jnp.float32, smallest / len(split), largest / len(split))
        gain = gain * jnp.repeat(jnp.exp(heights), dims[axis_at] // blocks).reshape((-1,) + (1,) * (len(dims) - 1 - axis_at))
    return gain


def bell_draw(key, shape, deviation, reach, shards=(), kind=jnp.bfloat16):
    factor_of = block_scale(key, shape, shards, -0.22, 0.18) if shards else 1.0
    entries = jax.random.normal(key, shape, jnp.float32) * deviation * factor_of
    return jnp.minimum(jnp.maximum(entries, -reach), reach).astype(kind)


def setup_inputs(seed: int = 0) -> dict:
    seeds = jax.random.split(jax.random.key(seed), 5)
    return {
        "left_factor": bell_draw(seeds[0], (S, C, N), 1.0, 6.0, ((0, 4), (2, 4))),
        "right_factor": bell_draw(seeds[1], (S, C, N), 1.0, 6.0, ((0, 4), (2, 8))),
        "out_weight": bell_draw(seeds[2], (CC, P_SIZE), 2.0, 12.0),
        "pair_cotangent": bell_draw(seeds[3], (N, N, P_SIZE), 0.05, 0.29882812, ((0, 16), (1, 8))),
    }


def reference(left_factor, right_factor, out_weight, pair_cotangent):
    seq_total = left_factor.shape[0]
    left_f = left_factor.astype(jnp.float32)
    right_f = right_factor.astype(jnp.float32)
    width = out_weight.shape[0]
    chans = left_factor.shape[1]
    pair_ch = out_weight.shape[1]
    tokens = left_factor.shape[2]
    blocks = tokens // TOK_ROW
    high = lax.Precision.HIGHEST

    def step(carry, block):
        wsum, rsum = carry
        first_row = (block * TOK_ROW).astype(jnp.int32)
        left_blk = lax.dynamic_slice_in_dim(left_f, first_row, TOK_ROW, 2)
        grad_blk = lax.dynamic_slice_in_dim(pair_cotangent, first_row, TOK_ROW, 0)
        outer = jnp.einsum('sci,sej->ijce', left_blk, right_f, precision=high) / seq_total
        outer = outer.reshape(TOK_ROW * tokens, width).astype(jnp.bfloat16)
        grad_two = grad_blk.reshape(TOK_ROW * tokens, pair_ch)
        delta = jnp.dot(grad_two, out_weight.T, preferred_element_type=jnp.float32).astype(jnp.bfloat16)
        wsum = wsum + jnp.dot(outer.T, grad_two, preferred_element_type=jnp.float32)
        delta_four = delta.astype(jnp.float32).reshape(TOK_ROW, tokens, chans, chans)
        left_blk_grad = jnp.einsum('ijce,sej->sci', delta_four, right_f, precision=high) / seq_total
        rsum = rsum + jnp.einsum('ijce,sci->sej', delta_four, left_blk, precision=high) / seq_total
        return (wsum, rsum), left_blk_grad

    start = (jnp.zeros((width, pair_ch), jnp.float32), jnp.zeros(right_f.shape, jnp.float32))
    (weight_grad, right_grad), pieces = lax.scan(step, start, jnp.arange(blocks, dtype=jnp.int32))
    left_grad = jnp.transpose(pieces, (1, 2, 0, 3)).reshape(seq_total, chans, tokens)
    return left_grad, right_grad, weight_grad
```

```python
import functools

import jax
import jax.numpy as jnp
from jax import lax
from jax.experimental import pallas as pl
from jax.experimental.pallas import tpu as pltpu
from jax.sharding import Mesh
from jax.sharding import PartitionSpec as P

BF16 = jnp.bfloat16
F32 = jnp.float32
COL = ("x", "yl")
DEPTH = ("yh", "core")
EVERY = ("yh", "core", "row", "x", "yl")
NT = (((1,), (1,)), ((), ()))
VMEM_LIMIT = 56 * 1024 * 1024


def vmem_spec():
    return pl.BlockSpec(memory_space=pltpu.VMEM)


def params():
    return pltpu.CompilerParams(vmem_limit_bytes=VMEM_LIMIT)


def cost(flops, moved):
    return pl.CostEstimate(flops=flops, bytes_accessed=moved, transcendentals=0)


def outer_kernel(bt_ref, a_ref, out_ref):
    out_ref[...] = jnp.dot(bt_ref[...], a_ref[...], preferred_element_type=F32).astype(BF16)


def outer_call(bt, ap):
    m, k = bt.shape
    n = ap.shape[1]
    tile = 512
    return pl.pallas_call(
        outer_kernel,
        grid=(n // tile,),
        in_specs=[pl.BlockSpec((m, k), lambda g: (0, 0)), pl.BlockSpec((k, tile), lambda g: (0, g))],
        out_specs=pl.BlockSpec((m, tile), lambda g: (0, g)),
        out_shape=jax.ShapeDtypeStruct((m, n), BF16),
        compiler_params=params(),
        cost_estimate=cost(2 * m * n * k, 2 * (m * n + m * k + k * n)),
        name="outer",
    )(bt, ap)


def place_pieces(me_ref, pieces, pairs_ref):
    rows = pieces[0].shape[1]
    for step, piece in enumerate(pieces):
        at = pl.multiple_of(jnp.bitwise_xor(me_ref[0], step) * rows, rows)
        pairs_ref[:, pl.ds(at, rows), :] = piece[...]


def left_kernel(chans, me_ref, g0, g1, g2, g3, w_ref, bp_ref, delta_ref, left_ref, pairs_ref):
    width = pairs_ref.shape[1]

    @pl.when(pl.program_id(0) == 0)
    def _():
        place_pieces(me_ref, (g0, g1, g2, g3), pairs_ref)

    here = w_ref.shape[0] // chans

    def step(t, carry):
        g = pairs_ref[pl.ds(2 * t, 2)].reshape(2 * width, -1)
        d = lax.dot_general(w_ref[...], g, NT, preferred_element_type=F32).astype(BF16)
        for u in range(2):
            rows = pl.ds(pl.multiple_of((2 * t + u) * chans, chans), chans)
            for c in range(here):
                delta_ref[rows, c * width : (c + 1) * width] = d[
                    c * chans : (c + 1) * chans, u * width : (u + 1) * width
                ]
        return carry

    lax.fori_loop(0, pairs_ref.shape[0] // 2, step, 0, unroll=4)
    left_ref[...] = jnp.dot(bp_ref[...], delta_ref[...], preferred_element_type=F32).astype(BF16)


def left_call(me, pieces, w, bp, chans):
    cols, rows, pair = pieces[0].shape
    width = 4 * rows
    seqs, k = bp.shape
    n = chans * width
    steps = 4
    tile = n // steps
    whole = pl.BlockSpec((cols, rows, pair), lambda g: (0, 0, 0))
    return pl.pallas_call(
        functools.partial(left_kernel, chans),
        grid=(steps,),
        in_specs=[
            pl.BlockSpec(memory_space=pltpu.SMEM),
            whole,
            whole,
            whole,
            whole,
            pl.BlockSpec((w.shape[0] // steps, pair), lambda g: (g, 0)),
            pl.BlockSpec((seqs, k), lambda g: (0, 0)),
        ],
        out_specs=[pl.BlockSpec((k, tile), lambda g: (0, g)), pl.BlockSpec((seqs, tile), lambda g: (0, g))],
        out_shape=[jax.ShapeDtypeStruct((k, n), BF16), jax.ShapeDtypeStruct((seqs, n), BF16)],
        scratch_shapes=[pltpu.VMEM((cols, width, pair), BF16)],
        compiler_params=params(),
        cost_estimate=cost(2 * k * n * (pair * 2 + seqs), 2 * (k * n + seqs * n + seqs * k)),
        name="left",
    )(me, *pieces, w, bp)


def right_kernel(a_ref, delta_ref, out_ref, acc_ref):
    g = pl.program_id(0)
    part = lax.dot_general(a_ref[...], delta_ref[...], NT, preferred_element_type=F32)

    @pl.when(g == 0)
    def _():
        acc_ref[...] = part

    @pl.when(g > 0)
    def _():
        acc_ref[...] += part

    @pl.when(g == pl.num_programs(0) - 1)
    def _():
        out_ref[...] = acc_ref[...].astype(BF16)


def right_call(ap, delta):
    seqs, k = ap.shape
    n = delta.shape[0]
    tile = 1024
    return pl.pallas_call(
        right_kernel,
        grid=(k // tile,),
        in_specs=[pl.BlockSpec((seqs, tile), lambda g: (0, g)), pl.BlockSpec((n, tile), lambda g: (0, g))],
        out_specs=pl.BlockSpec((seqs, n), lambda g: (0, 0)),
        out_shape=jax.ShapeDtypeStruct((seqs, n), BF16),
        scratch_shapes=[pltpu.VMEM((seqs, n), F32)],
        compiler_params=params(),
        cost_estimate=cost(2 * k * n * seqs, 2 * (k * n + seqs * n + seqs * k)),
        name="right",
    )(ap, delta)


def weight_kernel(chans, me_ref, g0, g1, g2, g3, outer_ref, out_ref, pairs_ref, acc_ref):
    step = pl.program_id(0)
    width = pairs_ref.shape[1]

    @pl.when(step == 0)
    def _():
        place_pieces(me_ref, (g0, g1, g2, g3), pairs_ref)
        acc_ref[...] = jnp.zeros_like(acc_ref)

    here = outer_ref.shape[0] // chans
    parts = []
    for u in range(here):
        rows = outer_ref[u * chans : (u + 1) * chans, :]
        parts.append(jnp.concatenate([rows[:, c * width : (c + 1) * width] for c in range(chans)], axis=0))
    g = pairs_ref[pl.ds(step * here, here)].reshape(here * width, -1)
    acc_ref[...] += jnp.dot(jnp.concatenate(parts, axis=1), g, preferred_element_type=F32)

    @pl.when(step == pl.num_programs(0) - 1)
    def _():
        out_ref[...] = acc_ref[...].astype(BF16)


def weight_call(me, pieces, outer, chans):
    cols, rows, pair = pieces[0].shape
    width = 4 * rows
    k, n = outer.shape
    here = 8
    whole = pl.BlockSpec((cols, rows, pair), lambda g: (0, 0, 0))
    return pl.pallas_call(
        functools.partial(weight_kernel, chans),
        grid=(cols // here,),
        in_specs=[
            pl.BlockSpec(memory_space=pltpu.SMEM),
            whole,
            whole,
            whole,
            whole,
            pl.BlockSpec((here * chans, n), lambda g: (g, 0)),
        ],
        out_specs=pl.BlockSpec((chans * chans, pair), lambda g: (0, 0)),
        out_shape=jax.ShapeDtypeStruct((chans * chans, pair), BF16),
        scratch_shapes=[pltpu.VMEM((cols, width, pair), BF16), pltpu.VMEM((chans * chans, pair), F32)],
        compiler_params=params(),
        cost_estimate=cost(4 * k * n * pair, 2 * k * n),
        name="weight",
    )(me, *pieces, outer)


def depth_exchange(array, other_chip, other_core):
    pairs = []
    for chip in range(2):
        for core in range(2):
            to = (chip ^ other_chip) * 2 + (core ^ other_core)
            pairs.append((chip * 2 + core, to))
    return lax.ppermute(array, DEPTH, pairs)


def summed(array, axes):
    peers = 1
    for axis in axes:
        peers *= lax.axis_size(axis)
    blocks = array.reshape(peers, array.shape[0] // peers, array.shape[1])
    blocks = lax.all_to_all(blocks, axes, 0, 0, tiled=True)
    return jnp.sum(blocks.astype(F32), axis=0)


def body(left_factor, right_factor, out_weight, pair_cotangent):
    seqs, chans, rows = left_factor.shape
    cols = right_factor.shape[2]
    scale = 1.0 / (seqs * lax.axis_size("yh") * lax.axis_size("core"))
    me = (lax.axis_index("yh") * 2 + lax.axis_index("core")).astype(jnp.int32).reshape(1)

    mine = jnp.transpose(pair_cotangent, (1, 0, 2))
    across = depth_exchange(mine, 1, 0)
    beside = depth_exchange(mine, 0, 1)
    both = depth_exchange(across, 0, 1)
    pieces = (mine, beside, across, both)

    ap = left_factor.reshape(seqs, chans * rows)
    bt = jnp.transpose(right_factor, (2, 1, 0)).reshape(cols * chans, seqs)
    bp = jnp.transpose(right_factor, (0, 2, 1)).reshape(seqs, cols * chans)

    outer = outer_call(bt, ap)
    delta, left_part = left_call(me, pieces, out_weight, bp, chans)
    right_part = right_call(ap, delta)
    weight_part = weight_call(me, pieces, outer, chans)

    left = summed(left_part, COL) * scale
    right = summed(right_part, ("row",)) * scale
    weight = summed(weight_part, EVERY) * scale
    left_grad = left.reshape(-1, chans, rows)
    right_grad = jnp.transpose(right.reshape(-1, cols, chans), (0, 2, 1))
    return left_grad, right_grad, weight


def solution(mesh):
    finer = Mesh(mesh.devices.reshape(2, 2, mesh.shape["row"], 4, 2), EVERY)
    in_specs = (P(DEPTH, None, "row"), P(DEPTH, None, COL), P(), P(("row",) + DEPTH, COL, None))
    out_specs = (P(DEPTH + COL, None, "row"), P(DEPTH + ("row",), None, COL), P(EVERY, None))
    return jax.shard_map(body, mesh=finer, in_specs=in_specs, out_specs=out_specs, check_vma=False)
```

```python
import functools

import jax
import jax.numpy as jnp
from jax import lax
from jax.experimental import pallas as pl
from jax.experimental.pallas import tpu as pltpu
from jax.sharding import Mesh
from jax.sharding import PartitionSpec as P

BF16 = jnp.bfloat16
F32 = jnp.float32
COL = ("x", "yl")
DEPTH = ("yh", "core")
EVERY = ("yh", "core", "row", "x", "yl")
NT = (((1,), (1,)), ((), ()))
CHUNKS = 8
VMEM_LIMIT = 56 * 1024 * 1024


def params():
    return pltpu.CompilerParams(vmem_limit_bytes=VMEM_LIMIT)


def cost(flops, moved):
    return pl.CostEstimate(flops=flops, bytes_accessed=moved, transcendentals=0)


def place_pieces(me_ref, pieces, pairs_ref):
    rows = pieces[0].shape[1]
    for step, piece in enumerate(pieces):
        at = pl.multiple_of(jnp.bitwise_xor(me_ref[0], step) * rows, rows)
        pairs_ref[:, pl.ds(at, rows), :] = piece[...]


def left_kernel(
    chans, me_ref, from_ref, g0, g1, g2, g3, w_ref, bt_ref,
    delta_ref, keep_a, send_a, keep_b, send_b, pairs_ref, turned_ref, b_ref,
):
    grid_step = pl.program_id(0)
    width = pairs_ref.shape[1]
    rows = bt_ref.shape[1] // 4

    @pl.when(grid_step == 0)
    def _():
        place_pieces(me_ref, (g0, g1, g2, g3), pairs_ref)
        for k in range(0, bt_ref.shape[0], 128):
            turned_ref[:, k : k + 128] = bt_ref[k : k + 128, :].T
        for q in range(4):
            start = pl.multiple_of(from_ref[q] * rows, 16)
            b_ref[q * rows : (q + 1) * rows, :] = turned_ref[pl.ds(start, rows), :]

    here = w_ref.shape[0] // chans
    many = 16

    def step(t, carry):
        g = pairs_ref[pl.ds(many * t, many)].reshape(many * width, -1)
        d = lax.dot_general(w_ref[...], g, NT, preferred_element_type=F32).astype(BF16)
        for u in range(many):
            at = pl.ds(pl.multiple_of((many * t + u) * chans, chans), chans)
            for c in range(here):
                delta_ref[at, c * width : (c + 1) * width] = d[
                    c * chans : (c + 1) * chans, u * width : (u + 1) * width
                ]
        return carry

    lax.fori_loop(0, pairs_ref.shape[0] // many, step, 0, unroll=2)
    total = jnp.dot(b_ref[...], delta_ref[...], preferred_element_type=F32).astype(BF16)
    tile = keep_a.shape[2]
    count = total.shape[1] // tile

    @pl.when(grid_step < 2)
    def _():
        for q in range(count):
            at = grid_step * count + q
            cut = slice(q * tile, (q + 1) * tile)
            keep_a[at] = total[: 2 * rows, cut]
            send_a[at] = total[2 * rows :, cut]

    @pl.when(grid_step >= 2)
    def _():
        for q in range(count):
            at = (grid_step - 2) * count + q
            cut = slice(q * tile, (q + 1) * tile)
            for half in range(2):
                low = 2 * half * rows
                keep_b[at, half * rows : (half + 1) * rows] = total[low : low + rows, cut]
                send_b[at, half * rows : (half + 1) * rows] = total[low + rows : low + 2 * rows, cut]


def left_call(me, source, pieces, w, bt, chans):
    cols, rows, pair = pieces[0].shape
    width = 4 * rows
    k, seqs = bt.shape
    n = chans * width
    steps = 4
    tile = n // steps
    whole = pl.BlockSpec((cols, rows, pair), lambda g: (0, 0, 0))
    smem = pl.BlockSpec(memory_space=pltpu.SMEM)
    part = (CHUNKS // 2, seqs // 2, n // CHUNKS)
    return pl.pallas_call(
        functools.partial(left_kernel, chans),
        grid=(steps,),
        in_specs=[
            smem,
            smem,
            whole,
            whole,
            whole,
            whole,
            pl.BlockSpec((w.shape[0] // steps, pair), lambda g: (g, 0)),
            pl.BlockSpec((k, seqs), lambda g: (0, 0)),
        ],
        out_specs=[pl.BlockSpec((k, tile), lambda g: (0, g))] + [pl.BlockSpec(part, lambda g: (0, 0, 0))] * 4,
        out_shape=[jax.ShapeDtypeStruct((k, n), BF16)] + [jax.ShapeDtypeStruct(part, BF16)] * 4,
        scratch_shapes=[
            pltpu.VMEM((cols, width, pair), BF16),
            pltpu.VMEM((seqs, k), BF16),
            pltpu.VMEM((seqs, k), BF16),
        ],
        compiler_params=params(),
        cost_estimate=cost(2 * k * n * (pair * 2 + seqs), 2 * (k * n + seqs * n + seqs * k)),
        name="left",
    )(me, source, *pieces, w, bt)


def right_kernel(from_ref, a_ref, delta_ref, keep_a, send_a, keep_b, send_b, acc_ref):
    g = pl.program_id(0)
    rows = a_ref.shape[0] // 4
    a = jnp.concatenate(
        [a_ref[pl.ds(pl.multiple_of(from_ref[q] * rows, 16), rows), :] for q in range(4)], axis=0
    )
    part = lax.dot_general(a, delta_ref[...], NT, preferred_element_type=F32)

    @pl.when(g == 0)
    def _():
        acc_ref[...] = part

    @pl.when(g > 0)
    def _():
        acc_ref[...] += part

    @pl.when(g == pl.num_programs(0) - 1)
    def _():
        half = keep_a.shape[1]
        keep_a[...] = acc_ref[: 2 * rows, :half].astype(BF16)
        send_a[...] = acc_ref[2 * rows :, :half].astype(BF16)
        for q in range(2):
            low = 2 * q * rows
            to = slice(q * rows, (q + 1) * rows)
            keep_b[to] = acc_ref[low : low + rows, half:].astype(BF16)
            send_b[to] = acc_ref[low + rows : low + 2 * rows, half:].astype(BF16)


def right_call(source, ap, delta):
    seqs, k = ap.shape
    n = delta.shape[0]
    tile = 1024
    part = (seqs // 2, n // 2)
    return pl.pallas_call(
        right_kernel,
        grid=(k // tile,),
        in_specs=[
            pl.BlockSpec(memory_space=pltpu.SMEM),
            pl.BlockSpec((seqs, tile), lambda g: (0, g)),
            pl.BlockSpec((n, tile), lambda g: (0, g)),
        ],
        out_specs=[pl.BlockSpec(part, lambda g: (0, 0))] * 4,
        out_shape=[jax.ShapeDtypeStruct(part, BF16)] * 4,
        scratch_shapes=[pltpu.VMEM((seqs, n), F32)],
        compiler_params=params(),
        cost_estimate=cost(2 * k * n * seqs, 2 * (k * n + seqs * n + seqs * k)),
        name="right",
    )(source, ap, delta)


def left_end_kernel(scale, keep_ref, came_ref, out_ref):
    chunks, _, tile = keep_ref.shape
    width = out_ref.shape[2]
    per = tile // width
    for q in range(chunks):
        total = (keep_ref[q] + came_ref[q].astype(F32)) * scale
        for c in range(per):
            out_ref[:, q * per + c, :] = total[:, c * width : (c + 1) * width]


def left_end_call(keep, came, chans, scale):
    chunks, seqs, tile = keep.shape
    return pl.pallas_call(
        functools.partial(left_end_kernel, scale),
        out_shape=jax.ShapeDtypeStruct((seqs, chans, chunks * tile // chans), F32),
        compiler_params=params(),
        cost_estimate=cost(2 * keep.size, 10 * keep.size),
        name="left_end",
    )(keep, came)


def right_end_kernel(scale, keep_a, came_a, keep_b, came_b, out_ref, turned_ref):
    chans, cols, seqs = out_ref.shape
    half = keep_a.shape[1]
    for at, (keep, came) in enumerate(((keep_a, came_a), (keep_b, came_b))):
        for k in range(0, half, 128):
            total = (keep[:, k : k + 128].astype(F32) + came[:, k : k + 128].astype(F32)) * scale
            turned_ref[at * half + k : at * half + k + 128, :] = total.T
    for e in range(chans):
        out_ref[e] = turned_ref[pl.ds(e, cols, stride=chans), :]


def right_end_call(keep_a, came_a, keep_b, came_b, chans, scale):
    seqs, half = keep_a.shape
    cols = 2 * half // chans
    return pl.pallas_call(
        functools.partial(right_end_kernel, scale),
        out_shape=jax.ShapeDtypeStruct((chans, cols, seqs), F32),
        scratch_shapes=[pltpu.VMEM((2 * half, seqs), F32)],
        compiler_params=params(),
        cost_estimate=cost(4 * keep_a.size, 16 * keep_a.size),
        name="right_end",
    )(keep_a, came_a, keep_b, came_b)


def weight_kernel(chans, me_ref, g0, g1, g2, g3, bt_ref, a_ref, out_ref, pairs_ref, acc_ref):
    step = pl.program_id(0)
    width = pairs_ref.shape[1]

    @pl.when(step == 0)
    def _():
        place_pieces(me_ref, (g0, g1, g2, g3), pairs_ref)
        acc_ref[...] = jnp.zeros_like(acc_ref)

    here = bt_ref.shape[0] // chans
    g = pairs_ref[pl.ds(step * here, here)].reshape(here * width, -1)
    group = 8
    for q in range(chans // group):
        a = a_ref[:, q * group * width : (q + 1) * group * width]
        outer = jnp.dot(bt_ref[...], a, preferred_element_type=F32).astype(BF16)
        parts = []
        for u in range(here):
            rows = outer[u * chans : (u + 1) * chans]
            parts.append(jnp.concatenate([rows[:, c * width : (c + 1) * width] for c in range(group)], axis=0))
        acc_ref[q * group * chans : (q + 1) * group * chans, :] += jnp.dot(
            jnp.concatenate(parts, axis=1), g, preferred_element_type=F32
        )

    @pl.when(step == pl.num_programs(0) - 1)
    def _():
        out_ref[...] = acc_ref[...].astype(BF16)


def weight_call(me, pieces, bt, ap, chans):
    cols, rows, pair = pieces[0].shape
    width = 4 * rows
    k, seqs = bt.shape
    n = ap.shape[1]
    here = 16
    whole = pl.BlockSpec((cols, rows, pair), lambda g: (0, 0, 0))
    return pl.pallas_call(
        functools.partial(weight_kernel, chans),
        grid=(cols // here,),
        in_specs=[
            pl.BlockSpec(memory_space=pltpu.SMEM),
            whole,
            whole,
            whole,
            whole,
            pl.BlockSpec((here * chans, seqs), lambda g: (g, 0)),
            pl.BlockSpec((seqs, n), lambda g: (0, 0)),
        ],
        out_specs=pl.BlockSpec((chans * chans, pair), lambda g: (0, 0)),
        out_shape=jax.ShapeDtypeStruct((chans * chans, pair), BF16),
        scratch_shapes=[pltpu.VMEM((cols, width, pair), BF16), pltpu.VMEM((chans * chans, pair), F32)],
        compiler_params=params(),
        cost_estimate=cost(2 * k * n * (seqs + 2 * pair), 2 * (k * seqs + n * seqs)),
        name="weight",
    )(me, *pieces, bt, ap)


def depth_exchange(array, other_chip, other_core):
    pairs = []
    for chip in range(2):
        for core in range(2):
            to = (chip ^ other_chip) * 2 + (core ^ other_core)
            pairs.append((chip * 2 + core, to))
    return lax.ppermute(array, DEPTH, pairs)


def ring_partner(at, bit):
    return at ^ 1 if bit == 0 else 3 - at


def ring_place(at, bits):
    for bit in (0, 1):
        if bits[bit]:
            at = ring_partner(at, bit)
    return at


def ring_sources(at):
    here = [ring_place(at, (first, second)) for first in (0, 1) for second in (0, 1)]
    return jnp.stack(here).astype(jnp.int32)


def swap(array, axis, bit=None):
    if bit is None:
        pairs = [(0, 1), (1, 0)]
    else:
        pairs = [(at, ring_partner(at, bit)) for at in range(4)]
    return lax.ppermute(array, axis, pairs)


def join(keep, came, dtype=BF16):
    return (keep.astype(F32) + came.astype(F32)).astype(dtype)


def summed(array, axes):
    peers = 1
    for axis in axes:
        peers *= lax.axis_size(axis)
    blocks = array.reshape(peers, array.shape[0] // peers, array.shape[1])
    blocks = lax.all_to_all(blocks, axes, 0, 0, tiled=True)
    return jnp.sum(blocks.astype(F32), axis=0)


def body(left_factor, right_factor, out_weight, pair_cotangent):
    seqs, chans, rows = left_factor.shape
    cols = right_factor.shape[2]
    scale = 1.0 / (seqs * lax.axis_size("yh") * lax.axis_size("core"))
    me = (lax.axis_index("yh") * 2 + lax.axis_index("core")).astype(jnp.int32).reshape(1)
    source_x = ring_sources(lax.axis_index("x"))
    source_z = ring_sources(lax.axis_index("row"))

    mine = jnp.transpose(pair_cotangent, (1, 0, 2))
    across = depth_exchange(mine, 1, 0)
    beside = depth_exchange(mine, 0, 1)
    ap = left_factor.reshape(seqs, chans * rows)
    bt = jnp.transpose(right_factor, (2, 1, 0)).reshape(cols * chans, seqs)
    across, ap, bt = lax.optimization_barrier((across, ap, bt))
    both = depth_exchange(across, 0, 1)
    pieces = (mine, beside, across, both)

    delta, keep_a, send_a, keep_b, send_b = left_call(me, source_x, pieces, out_weight, bt, chans)
    came = (swap(send_a, "x", 0), swap(send_b, "x", 1))
    weight_part = weight_call(me, pieces, bt, ap, chans)
    came, weight_part = lax.optimization_barrier((came, weight_part))

    cut = seqs // 4
    keep = (join(keep_a[:, :cut], came[0][:, :cut]), join(keep_b[:, :cut], came[1][:, :cut]))
    send = (join(keep_a[:, cut:], came[0][:, cut:]), join(keep_b[:, cut:], came[1][:, cut:]))
    came = (swap(send[0], "x", 1), swap(send[1], "x", 0))
    send, ap = lax.optimization_barrier((send, ap))
    right_parts = right_call(source_z, ap, delta)
    came, right_parts = lax.optimization_barrier((came, right_parts))
    keep_a, send_a, keep_b, send_b = right_parts
    right_came = (swap(send_a, "row", 0), swap(send_b, "row", 1))

    yl = lax.axis_index("yl")
    both_keep = [k.reshape(CHUNKS // 2, 2, cut // 2, -1) for k in keep]
    both_came = [c.reshape(CHUNKS // 2, 2, cut // 2, -1) for c in came]

    def take(at, dtype):
        parts = []
        for k, c in zip(both_keep, both_came):
            k = lax.dynamic_index_in_dim(k, at, 1, keepdims=False)
            c = lax.dynamic_index_in_dim(c, at, 1, keepdims=False)
            parts.append(join(k, c, dtype))
        return jnp.concatenate(parts, axis=0)

    left_came = swap(take(1 - yl, BF16), "yl")
    left_keep = take(yl, F32)

    send_end = (join(keep_a[cut:], right_came[0][cut:]), join(keep_b[cut:], right_came[1][cut:]))
    keep_end = (join(keep_a[:cut], right_came[0][:cut]), join(keep_b[:cut], right_came[1][:cut]))
    weight = summed(weight_part, EVERY) * scale
    right_last = (swap(send_end[0], "row", 1), swap(send_end[1], "row", 0))

    left_grad = left_end_call(left_keep, left_came, chans, scale)
    right_grad = right_end_call(keep_end[0], right_last[0], keep_end[1], right_last[1], chans, scale)
    return left_grad, jnp.transpose(right_grad, (2, 0, 1)), weight


def solution(mesh):
    finer = Mesh(mesh.devices.reshape(2, 2, mesh.shape["row"], 4, 2), EVERY)
    in_specs = (P(DEPTH, None, "row"), P(DEPTH, None, COL), P(), P(("row",) + DEPTH, COL, None))
    out_specs = (P(DEPTH + COL, None, "row"), P(DEPTH + ("row",), None, COL), P(EVERY, None))
    return jax.shard_map(body, mesh=finer, in_specs=in_specs, out_specs=out_specs, check_vma=False)
```

```python
import functools

import jax
import jax.numpy as jnp
from jax import lax
from jax.experimental import pallas as pl
from jax.experimental.pallas import tpu as pltpu
from jax.sharding import Mesh
from jax.sharding import PartitionSpec as P

BF16 = jnp.bfloat16
F32 = jnp.float32
COL = ("x", "yl")
DEPTH = ("yh", "core")
EVERY = ("yh", "core", "row", "x", "yl")
NT = (((1,), (1,)), ((), ()))
CHUNKS = 8
VMEM_LIMIT = 56 * 1024 * 1024


def params():
    return pltpu.CompilerParams(vmem_limit_bytes=VMEM_LIMIT)


def cost(flops, moved):
    return pl.CostEstimate(flops=flops, bytes_accessed=moved, transcendentals=0)


def place_pieces(me_ref, pieces, pairs_ref):
    rows = pieces[0].shape[1]
    for step, piece in enumerate(pieces):
        at = pl.multiple_of(jnp.bitwise_xor(me_ref[0], step) * rows, rows)
        pairs_ref[:, pl.ds(at, rows), :] = piece[...]


def pair_kernel(chans, me_ref, x_ref, z_ref, g0, g1, g2, g3, w_ref, bp_ref, a_ref, *rest):
    keep_a, send_a, keep_b, send_b = rest[:4]
    right_refs = rest[4:8]
    pairs_ref, b_ref, delta_ref = rest[8:]
    width = pairs_ref.shape[1]
    rows = bp_ref.shape[0] // 4
    place_pieces(me_ref, (g0, g1, g2, g3), pairs_ref)
    for q in range(4):
        start = pl.multiple_of(x_ref[q] * rows, 16)
        b_ref[q * rows : (q + 1) * rows, :] = bp_ref[pl.ds(start, rows), :]

    here = 8
    many = 16
    for first in range(0, chans, here):
        w = w_ref[first * chans : (first + here) * chans, :]

        def step(t, carry, w=w, first=first):
            g = pairs_ref[pl.ds(many * t, many)].reshape(many * width, -1)
            d = lax.dot_general(w, g, NT, preferred_element_type=F32).astype(BF16)
            for u in range(many):
                at = pl.ds(pl.multiple_of((many * t + u) * chans, chans), chans)
                for c in range(here):
                    delta_ref[at, (first + c) * width : (first + c + 1) * width] = d[
                        c * chans : (c + 1) * chans, u * width : (u + 1) * width
                    ]
            return carry

        lax.fori_loop(0, pairs_ref.shape[0] // many, step, 0, unroll=2)

    chunks, _, tile = keep_a.shape
    per = here * width // tile
    for at in range(0, 2 * chunks, per):
        total = jnp.dot(b_ref[...], delta_ref[:, at * tile : (at + per) * tile], preferred_element_type=F32)
        total = total.astype(BF16)
        for q in range(per):
            cut = slice(q * tile, (q + 1) * tile)
            if at < chunks:
                keep_a[at + q] = total[: 2 * rows, cut]
                send_a[at + q] = total[2 * rows :, cut]
            else:
                for half in range(2):
                    low = 2 * half * rows
                    to = slice(half * rows, (half + 1) * rows)
                    keep_b[at + q - chunks, to] = total[low : low + rows, cut]
                    send_b[at + q - chunks, to] = total[low + rows : low + 2 * rows, cut]

    strip = 512
    for at in range(0, delta_ref.shape[0], strip):
        a = jnp.concatenate(
            [a_ref[pl.ds(pl.multiple_of(z_ref[q] * rows, 16), rows), :] for q in range(4)], axis=0
        )
        part = lax.dot_general(a, delta_ref[at : at + strip, :], NT, preferred_element_type=F32)
        for q in range(4):
            right_refs[q][:, at : at + strip] = part[q * rows : (q + 1) * rows].astype(BF16)


def pair_call(me, source_x, source_z, pieces, w, bp, ap, chans):
    cols, rows, pair = pieces[0].shape
    width = 4 * rows
    seqs, k = bp.shape
    n = chans * width
    smem = pl.BlockSpec(memory_space=pltpu.SMEM)
    vmem = pl.BlockSpec(memory_space=pltpu.VMEM)
    left = (CHUNKS // 2, seqs // 2, n // CHUNKS)
    right = (seqs // 4, k)
    return pl.pallas_call(
        functools.partial(pair_kernel, chans),
        in_specs=[smem] * 3 + [vmem] * 7,
        out_specs=[vmem] * 8,
        out_shape=[jax.ShapeDtypeStruct(left, BF16)] * 4 + [jax.ShapeDtypeStruct(right, BF16)] * 4,
        scratch_shapes=[
            pltpu.VMEM((cols, width, pair), BF16),
            pltpu.VMEM((seqs, k), BF16),
            pltpu.VMEM((k, n), BF16),
        ],
        compiler_params=params(),
        cost_estimate=cost(2 * k * n * (pair * 2 + 2 * seqs), 2 * (2 * seqs * n + seqs * k)),
        name="pair",
    )(me, source_x, source_z, *pieces, w, bp, ap)


def left_end_kernel(scale, keep_a, came_a, keep_b, came_b, out_ref):
    chunks, _, tile = keep_a.shape
    width = out_ref.shape[2]
    per = tile // width
    for at, (keep, came) in enumerate(((keep_a, came_a), (keep_b, came_b))):
        for q in range(chunks):
            total = (keep[q].astype(F32) + came[q].astype(F32)) * scale
            for c in range(per):
                out_ref[:, (at * chunks + q) * per + c, :] = total[:, c * width : (c + 1) * width]


def left_end_call(keep, came, chans, scale):
    chunks, seqs, tile = keep[0].shape
    size = keep[0].size
    return pl.pallas_call(
        functools.partial(left_end_kernel, scale),
        out_shape=jax.ShapeDtypeStruct((seqs, chans, 2 * chunks * tile // chans), F32),
        compiler_params=params(),
        cost_estimate=cost(4 * size, 16 * size),
        name="left_end",
    )(keep[0], came[0], keep[1], came[1])


def right_end_kernel(scale, p0, p1, p2, p3, out_ref, turned_ref):
    chans, cols, _ = out_ref.shape
    for k in range(0, chans * cols, 128):
        parts = [p[:, k : k + 128].astype(F32) for p in (p0, p1, p2, p3)]
        total = ((parts[0] + parts[1]) + (parts[2] + parts[3])) * scale
        turned_ref[k : k + 128, :] = jnp.pad(total, ((0, 128 - total.shape[0]), (0, 0))).T
    for e in range(chans):
        out_ref[e] = turned_ref[pl.ds(e, cols, stride=chans), :][:, : out_ref.shape[2]]


def right_end_call(parts, chans, scale):
    seqs, n = parts[0].shape
    return pl.pallas_call(
        functools.partial(right_end_kernel, scale),
        out_shape=jax.ShapeDtypeStruct((chans, n // chans, seqs), F32),
        scratch_shapes=[pltpu.VMEM((n, 128), F32)],
        compiler_params=params(),
        cost_estimate=cost(4 * parts[0].size, 12 * parts[0].size),
        name="right_end",
    )(*parts)


def weight_kernel(chans, me_ref, g0, g1, g2, g3, bt_ref, a_ref, out_ref, pairs_ref, acc_ref):
    step = pl.program_id(0)
    width = pairs_ref.shape[1]

    @pl.when(step == 0)
    def _():
        place_pieces(me_ref, (g0, g1, g2, g3), pairs_ref)
        acc_ref[...] = jnp.zeros_like(acc_ref)

    here = bt_ref.shape[0] // chans
    g = pairs_ref[pl.ds(step * here, here)].reshape(here * width, -1)
    group = 8
    for q in range(chans // group):
        a = a_ref[:, q * group * width : (q + 1) * group * width]
        outer = jnp.dot(bt_ref[...], a, preferred_element_type=F32).astype(BF16)
        parts = []
        for u in range(here):
            rows = outer[u * chans : (u + 1) * chans]
            parts.append(jnp.concatenate([rows[:, c * width : (c + 1) * width] for c in range(group)], axis=0))
        acc_ref[q * group * chans : (q + 1) * group * chans, :] += jnp.dot(
            jnp.concatenate(parts, axis=1), g, preferred_element_type=F32
        )

    @pl.when(step == pl.num_programs(0) - 1)
    def _():
        out_ref[...] = acc_ref[...].astype(BF16)


def weight_call(me, pieces, bt, ap, chans):
    cols, rows, pair = pieces[0].shape
    width = 4 * rows
    k, seqs = bt.shape
    n = ap.shape[1]
    here = 16
    whole = pl.BlockSpec((cols, rows, pair), lambda g: (0, 0, 0))
    return pl.pallas_call(
        functools.partial(weight_kernel, chans),
        grid=(cols // here,),
        in_specs=[
            pl.BlockSpec(memory_space=pltpu.SMEM),
            whole,
            whole,
            whole,
            whole,
            pl.BlockSpec((here * chans, seqs), lambda g: (g, 0)),
            pl.BlockSpec((seqs, n), lambda g: (0, 0)),
        ],
        out_specs=pl.BlockSpec((chans * chans, pair), lambda g: (0, 0)),
        out_shape=jax.ShapeDtypeStruct((chans * chans, pair), BF16),
        scratch_shapes=[pltpu.VMEM((cols, width, pair), BF16), pltpu.VMEM((chans * chans, pair), F32)],
        compiler_params=params(),
        cost_estimate=cost(2 * k * n * (seqs + 2 * pair), 2 * (k * seqs + n * seqs)),
        name="weight",
    )(me, *pieces, bt, ap)


def depth_exchange(array, other_chip, other_core):
    pairs = []
    for chip in range(2):
        for core in range(2):
            to = (chip ^ other_chip) * 2 + (core ^ other_core)
            pairs.append((chip * 2 + core, to))
    return lax.ppermute(array, DEPTH, pairs)


def ring_partner(at, bit):
    return at ^ 1 if bit == 0 else 3 - at


def ring_place(at, bits):
    for bit in (0, 1):
        if bits[bit]:
            at = ring_partner(at, bit)
    return at


def ring_sources(at):
    here = [ring_place(at, (first, second)) for first in (0, 1) for second in (0, 1)]
    return jnp.stack(here).astype(jnp.int32)


def swap(array, axis, bit=None):
    if bit is None:
        pairs = [(0, 1), (1, 0)]
    else:
        pairs = [(at, ring_partner(at, bit)) for at in range(4)]
    return lax.ppermute(array, axis, pairs)


def join(keep, came, dtype=BF16):
    return (keep.astype(F32) + came.astype(F32)).astype(dtype)


def body(left_factor, right_factor, out_weight, pair_cotangent):
    seqs, chans, rows = left_factor.shape
    cols = right_factor.shape[2]
    scale = 1.0 / (seqs * lax.axis_size("yh") * lax.axis_size("core"))
    me = (lax.axis_index("yh") * 2 + lax.axis_index("core")).astype(jnp.int32).reshape(1)
    source_x = ring_sources(lax.axis_index("x"))
    source_z = ring_sources(lax.axis_index("row"))

    mine = jnp.transpose(pair_cotangent, (1, 0, 2))
    across = depth_exchange(mine, 1, 0)
    beside = depth_exchange(mine, 0, 1)
    ap = left_factor.reshape(seqs, chans * rows)
    bt = jnp.transpose(right_factor, (2, 1, 0)).reshape(cols * chans, seqs)
    bt = lax.optimization_barrier(bt)
    across, ap, bt, bp = lax.optimization_barrier((across, ap, bt, bt.T))
    both = depth_exchange(across, 0, 1)
    pieces = (mine, beside, across, both)

    keep_a, send_a, keep_b, send_b, *right_parts = pair_call(
        me, source_x, source_z, pieces, out_weight, bp, ap, chans
    )
    came_a, came_b = swap(send_a, "x", 0), swap(send_b, "x", 1)
    right_came = [right_parts[0]]
    for q in (3, 1, 2):
        pairs = [(at, ring_place(at, divmod(q, 2))) for at in range(4)]
        right_came.append(lax.ppermute(right_parts[q], "row", pairs))
    weight_part = weight_call(me, pieces, bt, ap, chans)
    came_a, came_b, right_came, weight_part = lax.optimization_barrier((came_a, came_b, right_came, weight_part))

    yl = lax.axis_index("yl")
    cut = seqs // 8

    def by_place(array):
        return array.reshape(CHUNKS // 2, 2, 2, cut, -1)

    keep_a, came_a, keep_b, came_b = by_place(keep_a), by_place(came_a), by_place(keep_b), by_place(came_b)

    def take(array, axis, at):
        return lax.dynamic_index_in_dim(array, at, axis, keepdims=False)

    send_b = join(keep_b[:, 1], came_b[:, 1])
    send_a = join(take(keep_a, 2, 1 - yl), take(came_a, 2, 1 - yl))
    came_b2 = swap(send_b, "x", 0)
    came_a2 = swap(send_a, "yl")
    keep_a = join(take(keep_a, 2, yl), take(came_a, 2, yl), F32)
    keep_b = join(keep_b[:, 0], came_b[:, 0], F32)
    keep_a, keep_b, weight_part = lax.optimization_barrier((keep_a, keep_b, weight_part))
    blocks = lax.all_to_all(weight_part.reshape(128, -1, weight_part.shape[1]), EVERY, 0, 0, tiled=True)
    right_grad = right_end_call(right_came, chans, scale)

    came_a = swap(join(keep_a[:, 1], came_a2[:, 1]), "x", 1)
    came_b = swap(join(take(keep_b, 1, 1 - yl), take(came_b2, 1, 1 - yl)), "yl")
    keep_a = join(keep_a[:, 0], came_a2[:, 0], F32)
    keep_b = join(take(keep_b, 1, yl), take(came_b2, 1, yl), F32)
    left_grad = left_end_call((keep_a, keep_b), (came_a, came_b), chans, scale)
    blocks, left_grad, right_grad = lax.optimization_barrier((blocks, left_grad, right_grad))
    weight = jnp.sum(blocks.astype(F32), axis=0) * scale
    return left_grad, jnp.transpose(right_grad, (2, 0, 1)), weight


def solution(mesh):
    finer = Mesh(mesh.devices.reshape(2, 2, mesh.shape["row"], 4, 2), EVERY)
    in_specs = (P(DEPTH, None, "row"), P(DEPTH, None, COL), P(), P(("row",) + DEPTH, COL, None))
    out_specs = (P(DEPTH + COL, None, "row"), P(DEPTH + ("row",), None, COL), P(EVERY, None))
    return jax.shard_map(body, mesh=finer, in_specs=in_specs, out_specs=out_specs, check_vma=False)
```

```python
import functools

import jax
import jax.numpy as jnp
from jax import lax
from jax.experimental import pallas as pl
from jax.experimental.pallas import tpu as pltpu
from jax.sharding import Mesh
from jax.sharding import PartitionSpec as P

BF16 = jnp.bfloat16
F32 = jnp.float32
COL = ("x", "yl")
DEPTH = ("yh", "core")
EVERY = ("yh", "core", "row", "x", "yl")
NT = (((1,), (1,)), ((), ()))
CHUNKS = 8
VMEM_LIMIT = 56 * 1024 * 1024


def params():
    return pltpu.CompilerParams(vmem_limit_bytes=VMEM_LIMIT)


def cost(flops, moved):
    return pl.CostEstimate(flops=flops, bytes_accessed=moved, transcendentals=0)


def piece_copies(me_ref, pieces, pairs_ref, sems):
    rows = pieces[0].shape[1]
    copies = []
    for step, piece in enumerate(pieces):
        at = pl.multiple_of(jnp.bitwise_xor(me_ref[0], step) * rows, rows)
        copies.append(pltpu.make_async_copy(piece, pairs_ref.at[:, pl.ds(at, rows), :], sems.at[step]))
    return copies


def row_copies(from_ref, source, target, sems):
    rows = source.shape[0] // 4
    copies = []
    for q in range(4):
        start = pl.multiple_of(from_ref[q] * rows, 16)
        copies.append(
            pltpu.make_async_copy(source.at[pl.ds(start, rows), :], target.at[q * rows : (q + 1) * rows, :], sems.at[q])
        )
    return copies


def pair_kernel(chans, me_ref, x_ref, z_ref, g0, g1, g2, g3, w_ref, bp_hbm, a_hbm, *rest):
    left_refs = rest[:4]
    right_refs = rest[4:8]
    pairs_ref, b_ref, a_ref, delta_ref = rest[8:12]
    keep_a, send_a, keep_b, send_b = rest[12:16]
    piece_sems, b_sems, a_sems, out_sems = rest[16:]
    width = pairs_ref.shape[1]
    rows = b_ref.shape[0] // 4
    piece_in = piece_copies(me_ref, (g0, g1, g2, g3), pairs_ref, piece_sems)
    b_in = row_copies(x_ref, bp_hbm, b_ref, b_sems)
    a_in = row_copies(z_ref, a_hbm, a_ref, a_sems)
    left_out = [
        pltpu.make_async_copy(part, out, out_sems.at[q])
        for q, (part, out) in enumerate(zip((keep_a, send_a, keep_b, send_b), left_refs))
    ]
    for copy in piece_in + b_in + a_in:
        copy.start()
    for copy in piece_in:
        copy.wait()

    here = 8
    many = 16
    for first in range(0, chans, here):
        w = w_ref[first * chans : (first + here) * chans, :]

        def step(t, carry, w=w, first=first):
            g = pairs_ref[pl.ds(many * t, many)].reshape(many * width, -1)
            d = lax.dot_general(w, g, NT, preferred_element_type=F32).astype(BF16)
            for u in range(many):
                at = pl.ds(pl.multiple_of((many * t + u) * chans, chans), chans)
                for c in range(here):
                    delta_ref[at, (first + c) * width : (first + c + 1) * width] = d[
                        c * chans : (c + 1) * chans, u * width : (u + 1) * width
                    ]
            return carry

        lax.fori_loop(0, pairs_ref.shape[0] // many, step, 0, unroll=2)

    for copy in b_in:
        copy.wait()
    chunks, _, tile = keep_a.shape
    per = here * width // tile
    for at in range(0, 2 * chunks, per):
        total = jnp.dot(b_ref[...], delta_ref[:, at * tile : (at + per) * tile], preferred_element_type=F32)
        total = total.astype(BF16)
        for q in range(per):
            cut = slice(q * tile, (q + 1) * tile)
            if at < chunks:
                keep_a[at + q] = total[: 2 * rows, cut]
                send_a[at + q] = total[2 * rows :, cut]
            else:
                for half in range(2):
                    low = 2 * half * rows
                    to = slice(half * rows, (half + 1) * rows)
                    keep_b[at + q - chunks, to] = total[low : low + rows, cut]
                    send_b[at + q - chunks, to] = total[low + rows : low + 2 * rows, cut]

        if at + per == chunks:
            left_out[0].start()
            left_out[1].start()
    left_out[2].start()
    left_out[3].start()

    for copy in a_in:
        copy.wait()
    strip = 512
    for at in range(0, delta_ref.shape[0], strip):
        part = lax.dot_general(a_ref[...], delta_ref[at : at + strip, :], NT, preferred_element_type=F32)
        for q in range(4):
            right_refs[q][:, at : at + strip] = part[q * rows : (q + 1) * rows].astype(BF16)
    for copy in left_out:
        copy.wait()


def pair_call(me, source_x, source_z, pieces, w, bp, ap, chans):
    cols, rows, pair = pieces[0].shape
    width = 4 * rows
    seqs, k = bp.shape
    n = chans * width
    smem = pl.BlockSpec(memory_space=pltpu.SMEM)
    vmem = pl.BlockSpec(memory_space=pltpu.VMEM)
    outside = pl.BlockSpec(memory_space=pl.ANY)
    left = (CHUNKS // 2, seqs // 2, n // CHUNKS)
    right = (seqs // 4, k)
    return pl.pallas_call(
        functools.partial(pair_kernel, chans),
        in_specs=[smem] * 3 + [outside] * 4 + [vmem] + [outside] * 2,
        out_specs=[outside] * 4 + [vmem] * 4,
        out_shape=[jax.ShapeDtypeStruct(left, BF16)] * 4 + [jax.ShapeDtypeStruct(right, BF16)] * 4,
        scratch_shapes=[
            pltpu.VMEM((cols, width, pair), BF16),
            pltpu.VMEM((seqs, k), BF16),
            pltpu.VMEM((seqs, n), BF16),
            pltpu.VMEM((k, n), BF16),
        ]
        + [pltpu.VMEM(left, BF16)] * 4
        + [pltpu.SemaphoreType.DMA((4,))] * 4,
        compiler_params=params(),
        cost_estimate=cost(2 * k * n * (pair * 2 + 2 * seqs), 2 * (2 * seqs * n + seqs * k)),
        name="pair",
    )(me, source_x, source_z, *pieces, w, bp, ap)


def left_end_kernel(scale, yl_ref, keep_a, came_a, last_a, keep_b, came_b, last_b, out_ref):
    _, chunks, _, tile = keep_a.shape
    width = out_ref.shape[2]
    per = tile // width
    for half, (keep, came, last) in enumerate(((keep_a, came_a, last_a), (keep_b, came_b, last_b))):
        at = yl_ref[0] if half else 0
        for q in range(chunks):
            total = (keep[at, q] + came[at, q].astype(F32) + last[q].astype(F32)) * scale
            for c in range(per):
                out_ref[:, (half * chunks + q) * per + c, :] = total[:, c * width : (c + 1) * width]


def left_end_call(yl, first, second, chans, scale):
    chunks, seqs, tile = first[2].shape
    size = first[2].size
    vmem = pl.BlockSpec(memory_space=pltpu.VMEM)
    return pl.pallas_call(
        functools.partial(left_end_kernel, scale),
        in_specs=[pl.BlockSpec(memory_space=pltpu.SMEM)] + [vmem] * 6,
        out_specs=vmem,
        out_shape=jax.ShapeDtypeStruct((seqs, chans, 2 * chunks * tile // chans), F32),
        compiler_params=params(),
        cost_estimate=cost(4 * size, 24 * size),
        name="left_end",
    )(yl, *first, *second)


def right_end_kernel(scale, p0, p1, p2, p3, out_ref, turned_ref):
    chans, cols, _ = out_ref.shape
    for k in range(0, chans * cols, 128):
        parts = [p[:, k : k + 128].astype(F32) for p in (p0, p1, p2, p3)]
        total = ((parts[0] + parts[1]) + (parts[2] + parts[3])) * scale
        turned_ref[k : k + 128, :] = jnp.pad(total, ((0, 128 - total.shape[0]), (0, 0))).T
    for e in range(chans):
        out_ref[e] = turned_ref[pl.ds(e, cols, stride=chans), :][:, : out_ref.shape[2]]


def right_end_call(parts, chans, scale):
    seqs, n = parts[0].shape
    return pl.pallas_call(
        functools.partial(right_end_kernel, scale),
        out_shape=jax.ShapeDtypeStruct((chans, n // chans, seqs), F32),
        scratch_shapes=[pltpu.VMEM((n, 128), F32)],
        compiler_params=params(),
        cost_estimate=cost(4 * parts[0].size, 12 * parts[0].size),
        name="right_end",
    )(*parts)


def weight_kernel(chans, me_ref, g0, g1, g2, g3, bt_hbm, a_hbm, out_ref, pairs_ref, bt_ref, a_ref, *sems):
    piece_sems, bt_sems, a_sems = sems
    width = pairs_ref.shape[1]
    groups = 4
    here = pairs_ref.shape[0] // groups
    group = chans // groups
    piece_in = piece_copies(me_ref, (g0, g1, g2, g3), pairs_ref, piece_sems)
    bt_in, a_in = [], []
    for q in range(groups):
        strip = slice(q * here * chans, (q + 1) * here * chans)
        bt_in.append(pltpu.make_async_copy(bt_hbm.at[strip, :], bt_ref.at[strip, :], bt_sems.at[q]))
        strip = slice(q * group * width, (q + 1) * group * width)
        a_in.append(pltpu.make_async_copy(a_hbm.at[:, strip], a_ref.at[:, strip], a_sems.at[q]))
    for copy in [bt_in[0], a_in[0]] + piece_in + bt_in[1:] + a_in[1:]:
        copy.start()
    for q in range(groups):
        a_in[q].wait()
        total = None
        for k in range(groups):
            if q == 0:
                bt_in[k].wait()
            bt = bt_ref[k * here * chans : (k + 1) * here * chans, :]
            a = a_ref[:, q * group * width : (q + 1) * group * width]
            outer = jnp.dot(bt, a, preferred_element_type=F32).astype(BF16)
            if q == 0 and k == 0:
                for copy in piece_in:
                    copy.wait()
            parts = []
            for u in range(here):
                rows = outer[u * chans : (u + 1) * chans]
                parts.append(jnp.concatenate([rows[:, c * width : (c + 1) * width] for c in range(group)], axis=0))
            g = pairs_ref[k * here : (k + 1) * here].reshape(here * width, -1)
            part = jnp.dot(jnp.concatenate(parts, axis=1), g, preferred_element_type=F32)
            total = part if total is None else total + part
        out_ref[q * group * chans : (q + 1) * group * chans, :] = total.astype(BF16)


def weight_call(me, pieces, bt, ap, chans):
    cols, rows, pair = pieces[0].shape
    width = 4 * rows
    k, seqs = bt.shape
    n = ap.shape[1]
    outside = pl.BlockSpec(memory_space=pl.ANY)
    return pl.pallas_call(
        functools.partial(weight_kernel, chans),
        in_specs=[pl.BlockSpec(memory_space=pltpu.SMEM)] + [outside] * 6,
        out_specs=pl.BlockSpec(memory_space=pltpu.VMEM),
        out_shape=jax.ShapeDtypeStruct((chans * chans, pair), BF16),
        scratch_shapes=[
            pltpu.VMEM((cols, width, pair), BF16),
            pltpu.VMEM((k, seqs), BF16),
            pltpu.VMEM((seqs, n), BF16),
        ]
        + [pltpu.SemaphoreType.DMA((4,))] * 3,
        compiler_params=params(),
        cost_estimate=cost(2 * k * n * (seqs + 2 * pair), 2 * (k * seqs + n * seqs)),
        name="weight",
    )(me, *pieces, bt, ap)


def depth_exchange(array, other_chip, other_core):
    pairs = []
    for chip in range(2):
        for core in range(2):
            to = (chip ^ other_chip) * 2 + (core ^ other_core)
            pairs.append((chip * 2 + core, to))
    return lax.ppermute(array, DEPTH, pairs)


def ring_partner(at, bit):
    return at ^ 1 if bit == 0 else 3 - at


def ring_place(at, bits):
    for bit in (0, 1):
        if bits[bit]:
            at = ring_partner(at, bit)
    return at


def ring_sources(at):
    here = [ring_place(at, (first, second)) for first in (0, 1) for second in (0, 1)]
    return jnp.stack(here).astype(jnp.int32)


def swap(array, axis, bit=None):
    if bit is None:
        pairs = [(0, 1), (1, 0)]
    else:
        pairs = [(at, ring_partner(at, bit)) for at in range(4)]
    return lax.ppermute(array, axis, pairs)


def join(keep, came, dtype=BF16):
    return (keep.astype(F32) + came.astype(F32)).astype(dtype)


def body(left_factor, right_factor, out_weight, pair_cotangent):
    seqs, chans, rows = left_factor.shape
    cols = right_factor.shape[2]
    scale = 1.0 / (seqs * lax.axis_size("yh") * lax.axis_size("core"))
    me = (lax.axis_index("yh") * 2 + lax.axis_index("core")).astype(jnp.int32).reshape(1)
    source_x = ring_sources(lax.axis_index("x"))
    source_z = ring_sources(lax.axis_index("row"))

    mine = jnp.transpose(pair_cotangent, (1, 0, 2))
    across = depth_exchange(mine, 1, 0)
    beside = depth_exchange(mine, 0, 1)
    ap = left_factor.reshape(seqs, chans * rows)
    bt = jnp.transpose(right_factor, (2, 1, 0)).reshape(cols * chans, seqs)
    bt = lax.optimization_barrier(bt)
    across, ap, bt, bp = lax.optimization_barrier((across, ap, bt, bt.T))
    both = depth_exchange(across, 0, 1)
    pieces = (mine, beside, across, both)

    keep_a, send_a, keep_b, send_b, *right_parts = pair_call(
        me, source_x, source_z, pieces, out_weight, bp, ap, chans
    )
    came_a, came_b = swap(send_a, "x", 0), swap(send_b, "x", 1)
    right_came = [right_parts[0]]
    for q in (3, 1, 2):
        pairs = [(at, ring_place(at, divmod(q, 2))) for at in range(4)]
        right_came.append(lax.ppermute(right_parts[q], "row", pairs))
    weight_part = weight_call(me, pieces, bt, ap, chans)
    came_a, came_b, right_came, weight_part = lax.optimization_barrier((came_a, came_b, right_came, weight_part))

    yl = lax.axis_index("yl")
    cut = seqs // 8

    def by_place(array):
        return array.reshape(CHUNKS // 2, 2, 2, cut, -1)

    keep_a, came_a, keep_b, came_b = by_place(keep_a), by_place(came_a), by_place(keep_b), by_place(came_b)

    def take(array, axis, at):
        return lax.dynamic_index_in_dim(array, at, axis, keepdims=False)

    send_b = join(keep_b[:, 1], came_b[:, 1])
    send_a = join(take(keep_a, 2, 1 - yl), take(came_a, 2, 1 - yl))
    came_b2 = swap(send_b, "x", 0)
    came_a2 = swap(send_a, "yl")
    keep_a = join(take(keep_a, 2, yl), take(came_a, 2, yl), F32)
    keep_b = join(keep_b[:, 0], came_b[:, 0], F32)
    keep_a, keep_b, weight_part = lax.optimization_barrier((keep_a, keep_b, weight_part))
    blocks = lax.all_to_all(weight_part.reshape(128, -1, weight_part.shape[1]), EVERY, 0, 0, tiled=True)
    right_grad = right_end_call(right_came, chans, scale)

    came_a = swap(join(keep_a[:, 1], came_a2[:, 1]), "x", 1)
    came_b = swap(join(take(keep_b, 1, 1 - yl), take(came_b2, 1, 1 - yl)), "yl")
    yl = yl.astype(jnp.int32).reshape(1)
    first = (jnp.swapaxes(keep_a, 0, 1), jnp.swapaxes(came_a2, 0, 1), came_a)
    second = (jnp.swapaxes(keep_b, 0, 1), jnp.swapaxes(came_b2, 0, 1), came_b)
    left_grad = left_end_call(yl, first, second, chans, scale)
    blocks, left_grad, right_grad = lax.optimization_barrier((blocks, left_grad, right_grad))
    weight = jnp.sum(blocks.astype(F32), axis=0) * scale
    return left_grad, jnp.transpose(right_grad, (2, 0, 1)), weight


def solution(mesh):
    finer = Mesh(mesh.devices.reshape(2, 2, mesh.shape["row"], 4, 2), EVERY)
    in_specs = (P(DEPTH, None, "row"), P(DEPTH, None, COL), P(), P(("row",) + DEPTH, COL, None))
    out_specs = (P(DEPTH + COL, None, "row"), P(DEPTH + ("row",), None, COL), P(EVERY, None))
    return jax.shard_map(body, mesh=finer, in_specs=in_specs, out_specs=out_specs, check_vma=False)
```
